32 devices in a mesh: row: 4 (over y, core), col: 8 (over z, x).
Axes of the slice: x: 2, y: 2, z: 4, core: 2. Of those that a mesh axis runs over, the one named last changes fastest.
Arguments:
- prior_solved: bfloat16 [92160, 768], P('col'), may hold values from -6 to 6
- lower_prior: bfloat16 [92160, 2, 3072], P('col', None, 'row'), may hold values from -0.01953125 to 0.01953125
- rhs: bfloat16 [2, 3072, 768], P(None, 'row'), may hold values from -6 to 6
- coupling: bfloat16 [3072, 3072], P('col', 'row'), may hold values from -0.109375 to 0.109375
- inverse_diag: bfloat16 [2, 3072, 3072], P(None, 'col', 'row'), may hold values from -1 to 1, as said below
Outputs:
- solved: bfloat16 [2, 3072, 768], P(None, 'row')
The draws below stay inside these ranges and needn't reach their ends.
Inputs may be any that keep to these rules, and one draw needn't show every extreme that they name: Each block inverse_diag[b] is the inverse of a unit lower triangular block: entry [b, j, i] is zero for j > i and exactly one for j == i.
All inputs are finite; a program needn't handle non-finite values.
Results may differ from the reference program's by a relative error of at most 0.0056.
Values may be sent and summed in bfloat16 or wider, within the bound.
A program may use at most 192 MiB of HBM per device.

```python
import math
import jax
import jax.numpy as jnp
from jax import lax

NB = 3072
RHS = 768
PRIOR = 92160


def draw_inverse_diag(key, part):
    noise_field = jax.random.normal(key, (2, NB, NB), jnp.float32)
    row_ids = lax.broadcasted_iota(jnp.int32, (NB, NB), 0)
    col_ids = lax.broadcasted_iota(jnp.int32, (NB, NB), 1)
    lower_mask = (row_ids < col_ids).astype(jnp.float32)
    unit_diag = (row_ids == col_ids).astype(jnp.float32)
    values = noise_field * lower_mask * (0.6 / math.sqrt(NB)) + unit_diag
    return values.astype(jnp.bfloat16)


def block_scale(rng, extent, split, least, high):
    def one(position, parts):
        draws = jax.random.uniform(jax.random.fold_in(jax.random.fold_in(rng, 6), position), (parts,), jnp.float32, least / len(split), high / len(split))
        return jnp.repeat(jnp.exp(draws), extent[position] // parts).reshape((-1,) + (1,) * (len(extent) - position - 1))

    loudness = one(*split[0])
    for cut in split[1:]:
        loudness = loudness * one(*cut)
    return loudness


def gaussian(key, shape, scale, reach, pieces=(), held_as=jnp.bfloat16):
    result = scale * jax.random.normal(key, shape, jnp.float32)
    if pieces:
        result = result * block_scale(key, shape, pieces, -0.22, 0.18)
    return jnp.clip(result, -reach, reach).astype(held_as)


def setup_inputs(seed: int = 0) -> dict:
    key_of = jax.random.split(jax.random.key(seed), 6)
    return {
        "prior_solved": gaussian(key_of[0], (PRIOR, RHS), 1.0, 6.0, ((0, 8),)),
        "lower_prior": gaussian(key_of[1], (PRIOR, 2, NB), PRIOR ** -0.5, 0.01953125, ((0, 8), (2, 4))),
        "rhs": gaussian(key_of[2], (2, NB, RHS), 1.0, 6.0, ((1, 4),)),
        "coupling": gaussian(key_of[3], (NB, NB), NB ** -0.5, 0.109375, ((0, 8), (1, 4))),
        "inverse_diag": draw_inverse_diag(jax.random.fold_in(key_of[5], 71), 0),
    }


def block_sum(lower_prior, prior_solved, block_id):
    return jnp.dot(lower_prior[:, block_id, :].T, prior_solved, preferred_element_type=jnp.float32)


def reference(prior_solved, lower_prior, rhs, coupling, inverse_diag):
    first_sum = block_sum(lower_prior, prior_solved, 0)
    second_sum = block_sum(lower_prior, prior_solved, 1)
    first_reduced = (rhs[0].astype(jnp.float32) - first_sum).astype(jnp.bfloat16)
    first_solved = jnp.dot(inverse_diag[0].T, first_reduced, preferred_element_type=jnp.float32).astype(jnp.bfloat16)
    cross_term = jnp.dot(coupling.T, first_solved, preferred_element_type=jnp.float32)
    second_reduced = (rhs[1].astype(jnp.float32) - second_sum - cross_term).astype(jnp.bfloat16)
    second_solved = jnp.dot(inverse_diag[1].T, second_reduced, preferred_element_type=jnp.float32).astype(jnp.bfloat16)
    return jnp.stack([first_solved, second_solved])
```

```python
import jax
import jax.numpy as jnp
from jax import lax
from jax.sharding import PartitionSpec as P


def product(left, right, left_dim):
    return lax.dot_general(
        left, right, (((left_dim,), (0,)), ((), ())), preferred_element_type=jnp.float32
    )


def on_device(prior_solved, lower_prior, rhs, coupling, inverse_diag):
    ncol = lax.axis_size("col")
    rows, width = rhs.shape[1], rhs.shape[2]
    share = width // ncol
    share_start = lax.axis_index("col") * share
    first_inverse = lax.all_gather(inverse_diag[0], "col", axis=0, tiled=True)
    whole_coupling = lax.all_gather(coupling, "col", axis=0, tiled=True)
    second_inverse = lax.all_gather(inverse_diag[1], "col", axis=0, tiled=True)
    rhs_share = lax.dynamic_slice_in_dim(rhs, share_start, share, 2).astype(jnp.float32)
    rhs_share = rhs_share.transpose(0, 2, 1)
    terms = product(lower_prior, prior_solved, 0).astype(jnp.bfloat16)
    terms = terms.transpose(2, 0, 1).reshape(ncol, share, 2, rows).transpose(0, 2, 1, 3)
    swapped = lax.all_to_all(terms, "col", 0, 0, tiled=True)
    shares = jnp.sum(swapped.astype(jnp.float32), axis=0)

    def apply_share(vector_rows, left_block):
        full_vector = lax.all_gather(vector_rows, "row", axis=1, tiled=True)
        return product(full_vector, left_block, 1)

    first_reduced = (rhs_share[0] - shares[0]).astype(jnp.bfloat16)
    first_solved = apply_share(first_reduced, first_inverse).astype(jnp.bfloat16)
    cross_term = apply_share(first_solved, whole_coupling)
    second_reduced = (rhs_share[1] - shares[1] - cross_term).astype(jnp.bfloat16)
    second_solved = apply_share(second_reduced, second_inverse).astype(jnp.bfloat16)
    first_out = lax.all_gather(first_solved, "col", axis=0, tiled=True)
    second_out = lax.all_gather(second_solved, "col", axis=0, tiled=True)
    return jnp.stack([first_out.T, second_out.T])


def solution(mesh):
    return jax.shard_map(
        on_device,
        mesh=mesh,
        in_specs=(
            P("col", None),
            P("col", None, "row"),
            P(None, "row", None),
            P("col", "row"),
            P(None, "col", "row"),
        ),
        out_specs=P(None, "row", None),
        check_vma=False,
    )
```
